32 devices in a mesh: replica: 8 (over y, x, core), fsdp: 4 (over z).
Axes of the slice: x: 2, y: 2, z: 4, core: 2. Of those that a mesh axis runs over, the one named last changes fastest.
Arguments:
- inputs: bfloat16 [2, 4096, 4096], P(None, ('replica', 'fsdp')), may hold values from -6 to 6
- cotangents: bfloat16 [2, 4096, 512], P(None, ('replica', 'fsdp')), may hold values from -1.0546875 to 1.0546875
- weights: float32 [8, 4096, 512], P('replica', 'fsdp'), may hold values from -6 to 6
- first_moment: bfloat16 [8, 4096, 512], P('replica', 'fsdp'), may hold values from -6 to 6
- second_moment: bfloat16 [8, 4096, 512], P('replica', 'fsdp'), may hold values from 0.5 to 8
- anchor: float32 [4096, 512], P('fsdp'), may hold values from -6 to 6
- outer_momentum: float32 [4096, 512], P('fsdp'), may hold values from -3 to 3
Outputs:
- weights_out: float32 [8, 4096, 512], P('replica', 'fsdp')
- first_out: bfloat16 [8, 4096, 512], P('replica', 'fsdp')
- second_out: bfloat16 [8, 4096, 512], P('replica', 'fsdp')
- anchor_out: float32 [4096, 512], P('fsdp')
- momentum_out: float32 [4096, 512], P('fsdp')
The draws below stay inside these ranges and needn't reach their ends.
All inputs are finite; a program needn't handle non-finite values.
Results may differ from the reference program's by a relative error of at most 0.008.
Values may be sent and summed in bfloat16 or wider, within the bound.
A program may use at most 64 MiB of HBM per device.

```python
import math
import jax
import jax.numpy as jnp
from jax import lax

DIN = 4096
F = 512
TOK_DEV = 128
STEPS = 2
REPLICAS = 8
TOK_REP = 512
TOKENS = 4096
N_FSDP = 4


def shard_levels(rng, extent, shards, low, largest):
    def one(position, shards_of):
        steps = jax.random.uniform(jax.random.fold_in(jax.random.fold_in(rng, 6), position), (shards_of,), jnp.float32, low / len(shards), largest / len(shards))
        return jnp.repeat(jnp.exp(steps), extent[position] // shards_of).reshape((-1,) + (1,) * (len(extent) - position - 1))

    factor_of = one(*shards[0])
    for cut in shards[1:]:
        factor_of = factor_of * one(*cut)
    return factor_of


def bell_draw(stream_key, shape, spread, reach, cuts=(), kind=jnp.bfloat16):
    drawn = spread * jax.random.normal(stream_key, shape, jnp.float32)
    if cuts:
        drawn = drawn * shard_levels(stream_key, shape, cuts, -0.22, 0.18)
    return jnp.clip(drawn, -reach, reach).astype(kind)


def setup_inputs(seed: int = 0) -> dict:
    key_of = jax.random.split(jax.random.key(seed), 8)
    inputs = bell_draw(key_of[0], (STEPS, TOKENS, DIN), 1.0, 6.0, ((1, 32),))
    cotangents = bell_draw(key_of[1], (STEPS, TOKENS, F), (4.0 / (TOK_DEV * N_FSDP) ** 0.5), 1.0546875, ((1, 32),))
    weights = bell_draw(key_of[2], (REPLICAS, DIN, F), 1.0, 6.0, ((0, 8), (1, 4)), jnp.float32)
    first_moment = bell_draw(key_of[3], (REPLICAS, DIN, F), 1.0, 6.0, ((0, 8), (1, 4)))
    second_moment = jnp.clip(jnp.exp(math.log(8.0) - 2.7725887 * jax.random.uniform(key_of[4], (REPLICAS, DIN, F), jnp.float32) ** shard_levels(key_of[4], (REPLICAS, DIN, F), ((0, 8), (1, 4)), -0.2, 0.2)), 0.5, 8.0).astype(jnp.bfloat16)
    anchor = bell_draw(key_of[5], (DIN, F), 1.0, 6.0, ((0, 4),), jnp.float32)
    outer_momentum = bell_draw(key_of[6], (DIN, F), 0.5, 3.0, ((0, 4),), jnp.float32)
    return {"inputs": inputs, "cotangents": cotangents, "weights": weights, "first_moment": first_moment, "second_moment": second_moment, "anchor": anchor, "outer_momentum": outer_momentum}


BETA_FIRST = 0.9
BETA_SECOND = 0.95
INNER_RATE = 0.01
WEIGHT_DECAY = 0.1
EPSILON = 1e-08
OUTER_RATE = 0.7
MOMENTUM_KEEP = 0.9
MERGE_WEIGHT = 0.5

def inner_update(weight, first_moment, second_moment, gradient):
    first_new = (BETA_FIRST * first_moment.astype(jnp.float32) + (1.0 - BETA_FIRST) * gradient).astype(jnp.bfloat16)
    second_new = (BETA_SECOND * second_moment.astype(jnp.float32) + (1.0 - BETA_SECOND) * gradient * gradient).astype(jnp.bfloat16)
    first_kept, second_kept = lax.optimization_barrier((first_new, second_new))
    first_read = first_kept.astype(jnp.float32)
    second_read = second_kept.astype(jnp.float32)
    weight_new = weight - INNER_RATE * (first_read / (jnp.sqrt(second_read) + EPSILON) + WEIGHT_DECAY * weight)
    return (weight_new, first_new, second_new)

def reference(inputs, cotangents, weights, first_moment, second_moment, anchor, outer_momentum):
    pseudo = lax.optimization_barrier(jnp.sum(anchor[None] - weights, axis=0)) / REPLICAS
    momentum_out = MOMENTUM_KEEP * outer_momentum + pseudo
    anchor_out = anchor - OUTER_RATE * (pseudo + MOMENTUM_KEEP * momentum_out)

    def one_worker(packed):
        worker, weight, first_state, second_state = packed
        start = (worker * TOK_REP).astype(jnp.int32)
        for which in range(STEPS):
            features = lax.dynamic_slice_in_dim(inputs[which], start, TOK_REP, 0)
            upstream = lax.dynamic_slice_in_dim(cotangents[which], start, TOK_REP, 0)
            gradient = lax.dot_general(features, upstream, (((0,), (0,)), ((), ())), preferred_element_type=jnp.float32)
            weight, first_state, second_state = inner_update(weight, first_state, second_state, gradient)
            if which == 0:
                weight = MERGE_WEIGHT * weight + (1.0 - MERGE_WEIGHT) * anchor_out
        return (weight, first_state, second_state)
    workers = jnp.arange(REPLICAS, dtype=jnp.int32)
    weights_out, first_out, second_out = lax.map(one_worker, (workers, weights, first_moment, second_moment))
    return (weights_out, first_out, second_out, anchor_out, momentum_out)
```

```python
import functools

import jax
import jax.numpy as jnp
from jax import lax
from jax.experimental import pallas as pl
from jax.experimental.pallas import tpu as pltpu
from jax.sharding import PartitionSpec as P

MESH = pl.DeviceIdType.MESH
F32 = jnp.float32
BF16 = jnp.bfloat16

BETA_FIRST = 0.9
BETA_SECOND = 0.95
INNER_RATE = 0.01
WEIGHT_DECAY = 0.1
EPSILON = 1e-08
OUTER_RATE = 0.7
MOMENTUM_KEEP = 0.9
MERGE_WEIGHT = 0.5


def greet(n, workers):
    barrier = pltpu.get_barrier_semaphore()
    me, worker = lax.axis_index("fsdp"), lax.axis_index("replica")
    for step in range(1, n):
        pl.semaphore_signal(
            barrier, inc=1, device_id=(worker, lax.rem(me + step, n)), device_id_type=MESH
        )
    for step in range(1, workers):
        pl.semaphore_signal(
            barrier, inc=1, device_id=(lax.rem(worker + step, workers), me), device_id_type=MESH
        )
    pl.semaphore_wait(barrier, n - 1 + workers - 1)


def exchange_kernel(n, workers, *refs):
    if workers > 1:
        (x_ref, y_ref, w_ref, a_ref, xg_ref, yg_ref, p_ref, w_vmem, a_vmem, slots, mean,
         x_send, x_recv, y_send, y_recv, own_sem, load_sem, d_send, d_recv, p_send, p_recv) = refs
    else:
        x_ref, y_ref, xg_ref, yg_ref, x_send, x_recv, y_send, y_recv, own_sem = refs
    me, worker = lax.axis_index("fsdp"), lax.axis_index("replica")
    steps, tok, din = x_ref.shape
    rows = din // n

    if workers > 1:
        load_w = pltpu.make_async_copy(w_ref, w_vmem, load_sem.at[0])
        load_a = pltpu.make_async_copy(a_ref, a_vmem, load_sem.at[1])
        load_w.start()
        load_a.start()
    greet(n, workers)

    token_rows = pl.ds(pl.multiple_of(me * tok, tok), tok)
    order = sorted(range(1, n), key=lambda d: (abs(2 * d - n), d))
    sends = []
    for s in range(steps):
        for d in order:
            peer = lax.rem(me + d, n)
            sends.append(pltpu.make_async_remote_copy(
                src_ref=y_ref.at[s], dst_ref=yg_ref.at[s, token_rows],
                send_sem=y_send.at[s, d - 1], recv_sem=y_recv.at[s, d - 1],
                device_id=(worker, peer), device_id_type=MESH))
            sends.append(pltpu.make_async_remote_copy(
                src_ref=x_ref.at[s, :, pl.ds(pl.multiple_of(peer * rows, rows), rows)],
                dst_ref=xg_ref.at[s, token_rows],
                send_sem=x_send.at[s, d - 1], recv_sem=x_recv.at[s, d - 1],
                device_id=(worker, peer), device_id_type=MESH))
    for copy in sends:
        copy.start()
    own_x = pltpu.make_async_copy(
        x_ref.at[:, :, pl.ds(pl.multiple_of(me * rows, rows), rows)],
        xg_ref.at[:, token_rows], own_sem.at[0])
    own_y = pltpu.make_async_copy(y_ref, yg_ref.at[:, token_rows], own_sem.at[1])
    own_x.start()
    own_y.start()

    if workers > 1:
        part = rows // workers
        mine = pl.ds(pl.multiple_of(worker * part, part), part)
        load_w.wait()
        load_a.wait()
        a_vmem[...] = a_vmem[...] - w_vmem[...]
        drifts, means = [], []
        for d in range(1, workers):
            peer = lax.rem(worker + d, workers)
            drifts.append(pltpu.make_async_remote_copy(
                src_ref=a_vmem.at[pl.ds(pl.multiple_of(peer * part, part), part)],
                dst_ref=slots.at[d - 1],
                send_sem=d_send.at[d - 1], recv_sem=d_recv.at[d - 1],
                device_id=(peer, me), device_id_type=MESH))
        for copy in drifts:
            copy.start()
        for copy in drifts:
            copy.wait_recv()
        summed = a_vmem[mine]
        for d in range(1, workers):
            summed = summed + slots[d - 1]
        mean[...] = summed / workers
        for d in range(1, workers):
            peer = lax.rem(worker + d, workers)
            means.append(pltpu.make_async_remote_copy(
                src_ref=mean, dst_ref=p_ref.at[mine],
                send_sem=p_send.at[d - 1], recv_sem=p_recv.at[d - 1],
                device_id=(peer, me), device_id_type=MESH))
        for copy in means:
            copy.start()
        own_p = pltpu.make_async_copy(mean, p_ref.at[mine], own_sem.at[2])
        own_p.start()
        for copy in drifts:
            copy.wait_send()
        for copy in means:
            copy.wait()
        own_p.wait()
    own_x.wait()
    own_y.wait()
    for copy in sends:
        copy.wait()


def exchange(n, workers, inputs, cotangents, weight, anchor):
    steps, tok, din = inputs.shape
    width = cotangents.shape[2]
    rows = din // n
    outs = [
        jax.ShapeDtypeStruct((steps, n * tok, rows), inputs.dtype),
        jax.ShapeDtypeStruct((steps, n * tok, width), cotangents.dtype),
    ]
    operands = [inputs, cotangents]
    near = pltpu.SemaphoreType.DMA((steps, n - 1))
    scratch = [near] * 4 + [pltpu.SemaphoreType.DMA((3,))]
    if workers > 1:
        part = rows // workers
        far = pltpu.SemaphoreType.DMA((workers - 1,))
        outs.append(jax.ShapeDtypeStruct((rows, width), F32))
        operands += [weight, anchor]
        scratch = [
            pltpu.VMEM((rows, width), F32),
            pltpu.VMEM((rows, width), F32),
            pltpu.VMEM((workers - 1, part, width), F32),
            pltpu.VMEM((part, width), F32),
        ] + scratch + [pltpu.SemaphoreType.DMA((2,))] + [far] * 4
    return pl.pallas_call(
        functools.partial(exchange_kernel, n, workers),
        out_shape=outs,
        in_specs=[pl.BlockSpec(memory_space=pl.ANY)] * len(operands),
        out_specs=[pl.BlockSpec(memory_space=pl.ANY)] * len(outs),
        scratch_shapes=scratch,
        compiler_params=pltpu.CompilerParams(
            collective_id=0, has_side_effects=True, vmem_limit_bytes=16 * 2**20
        ),
        name="exchange",
    )(*operands)


def update_kernel(x_ref, y_ref, w_ref, m_ref, v_ref, a_ref, o_ref, p_ref,
                  w_out, m_out, v_out, a_out, o_out):
    anchor, pseudo = a_ref[...], p_ref[...]
    momentum = MOMENTUM_KEEP * o_ref[...] + pseudo
    anchor_new = anchor - OUTER_RATE * (pseudo + MOMENTUM_KEEP * momentum)
    o_out[...] = momentum
    a_out[...] = anchor_new
    weight, first, second = w_ref[0], m_ref[0], v_ref[0]
    for s in range(x_ref.shape[0]):
        gradient = lax.dot_general(
            x_ref[s], y_ref[s], (((0,), (0,)), ((), ())), preferred_element_type=F32
        )
        first = (BETA_FIRST * first.astype(F32) + (1.0 - BETA_FIRST) * gradient).astype(BF16)
        second = (
            BETA_SECOND * second.astype(F32) + (1.0 - BETA_SECOND) * gradient * gradient
        ).astype(BF16)
        weight = weight - INNER_RATE * (
            first.astype(F32) / (jnp.sqrt(second.astype(F32)) + EPSILON) + WEIGHT_DECAY * weight
        )
        if s == 0:
            weight = MERGE_WEIGHT * weight + (1.0 - MERGE_WEIGHT) * anchor_new
    w_out[0] = weight
    m_out[0] = first
    v_out[0] = second


def update(gathered, upstream, weights, first, second, anchor, outer, pseudo):
    steps, tokens, rows = gathered.shape
    width = upstream.shape[2]
    block = min(128, rows)
    state = pl.BlockSpec((1, block, width), lambda i: (0, i, 0))
    plain = pl.BlockSpec((block, width), lambda i: (i, 0))
    shape = lambda ref: jax.ShapeDtypeStruct(ref.shape, ref.dtype)
    return pl.pallas_call(
        update_kernel,
        grid=(rows // block,),
        in_specs=[
            pl.BlockSpec((steps, tokens, block), lambda i: (0, 0, i)),
            pl.BlockSpec((steps, tokens, width), lambda i: (0, 0, 0)),
            state, state, state, plain, plain, plain,
        ],
        out_specs=[state, state, state, plain, plain],
        out_shape=[shape(weights), shape(first), shape(second), shape(anchor), shape(outer)],
        compiler_params=pltpu.CompilerParams(vmem_limit_bytes=40 * 2**20),
        name="update",
    )(gathered, upstream, weights, first, second, anchor, outer, pseudo)


def solution(mesh):
    n, workers = mesh.shape["fsdp"], mesh.shape["replica"]

    def body(inputs, cotangents, weights, first, second, anchor, outer):
        rows = anchor.shape[0]
        if rows % (16 * workers) == 0:
            gathered, upstream, pseudo = exchange(
                n, workers, inputs, cotangents, weights[0], anchor
            )
        else:
            gathered, upstream = exchange(n, 1, inputs, cotangents, None, None)
            pseudo = lax.psum(anchor - weights[0], "replica") / workers
        return tuple(update(gathered, upstream, weights, first, second, anchor, outer, pseudo))

    in_specs = (
        P(None, ("replica", "fsdp"), None),
        P(None, ("replica", "fsdp"), None),
        P("replica", "fsdp", None),
        P("replica", "fsdp", None),
        P("replica", "fsdp", None),
        P("fsdp", None),
        P("fsdp", None),
    )
    out_specs = (
        P("replica", "fsdp", None),
        P("replica", "fsdp", None),
        P("replica", "fsdp", None),
        P("fsdp", None),
        P("fsdp", None),
    )
    return jax.shard_map(body, mesh=mesh, in_specs=in_specs, out_specs=out_specs, check_vma=False)
```

```python
import functools

import jax
import jax.numpy as jnp
from jax import lax
from jax.experimental import pallas as pl
from jax.experimental.pallas import tpu as pltpu
from jax.sharding import PartitionSpec as P

MESH = pl.DeviceIdType.MESH
F32 = jnp.float32
BF16 = jnp.bfloat16

BETA_FIRST = 0.9
BETA_SECOND = 0.95
INNER_RATE = 0.01
WEIGHT_DECAY = 0.1
EPSILON = 1e-08
OUTER_RATE = 0.7
MOMENTUM_KEEP = 0.9
MERGE_WEIGHT = 0.5
EXCHANGE_VMEM = 60 * 2**20
UPDATE_VMEM = 60 * 2**20


def greet(n, workers):
    barrier = pltpu.get_barrier_semaphore()
    me, worker = lax.axis_index("fsdp"), lax.axis_index("replica")
    for step in range(1, n):
        pl.semaphore_signal(
            barrier, inc=1, device_id=(worker, lax.rem(me + step, n)), device_id_type=MESH
        )
    for step in range(1, workers):
        pl.semaphore_signal(
            barrier, inc=1, device_id=(lax.rem(worker + step, workers), me), device_id_type=MESH
        )
    pl.semaphore_wait(barrier, n - 1 + workers - 1)


def partner(me, k, n):
    if n & (n - 1):
        return lax.rem(me + k, n)
    peer, bit = me, 1
    while bit < n:
        if k & bit:
            peer = peer + (1 - 2 * (me // bit % 2)) * bit
        bit *= 2
    return peer


def exchange_kernel(n, workers, *refs):
    if workers > 1:
        (x_ref, y_ref, w_ref, a_ref, xg_ref, yg_ref, p_ref, w_vmem, a_vmem, slots, mean,
         x_send, x_recv, y_send, y_recv, own_sem, load_sem, d_send, d_recv, p_send, p_recv) = refs
    else:
        x_ref, y_ref, xg_ref, yg_ref, x_send, x_recv, y_send, y_recv, own_sem = refs
    me, worker = lax.axis_index("fsdp"), lax.axis_index("replica")
    steps, tok, din = x_ref.shape
    rows = din // n

    if workers > 1:
        load_w = pltpu.make_async_copy(w_ref, w_vmem, load_sem.at[0])
        load_a = pltpu.make_async_copy(a_ref, a_vmem, load_sem.at[1])
        load_w.start()
        load_a.start()
    greet(n, workers)

    token_rows = pl.ds(pl.multiple_of(me * tok, tok), tok)
    right, left = lax.rem(me + 1, n), lax.rem(me + n - 1, n)

    def hop(h, way):
        to_right = way == 0
        origin = me - (h - 1) if to_right else me + (h - 1)
        sends_it = jnp.logical_and(origin >= 0, me < n - 1) if to_right else jnp.logical_and(
            origin < n, me > 0)
        comes = me >= h if to_right else me + h < n
        held = pl.ds(pl.multiple_of(lax.rem(origin + n, n) * tok, tok), tok)
        copy = pltpu.make_async_remote_copy(
            src_ref=y_ref if h == 1 else yg_ref.at[:, held], dst_ref=yg_ref.at[:, held],
            send_sem=y_send.at[way, h - 1], recv_sem=y_recv.at[way, h - 1],
            device_id=(worker, right if to_right else left), device_id_type=MESH)
        return copy, sends_it, comes

    def hop_start(h):
        for way in range(2):
            copy, sends_it, _ = hop(h, way)
            pl.when(sends_it)(copy.start)

    def hop_arrived(h):
        for way in range(2):
            copy, _, comes = hop(h, way)
            pl.when(comes)(copy.wait_recv)

    def pass_on():
        for h in range(3, n):
            hop_arrived(h - 1)
            hop_start(h)

    hop_start(1)
    sends = []
    for k in range(n - 1, 0, -1):
        for s in range(steps):
            peer = partner(me, k, n)
            sends.append(pltpu.make_async_remote_copy(
                src_ref=x_ref.at[s, :, pl.ds(pl.multiple_of(peer * rows, rows), rows)],
                dst_ref=xg_ref.at[s, token_rows],
                send_sem=x_send.at[s, k - 1], recv_sem=x_recv.at[s, k - 1],
                device_id=(worker, peer), device_id_type=MESH))
    for copy in sends:
        copy.start()
    own_x = pltpu.make_async_copy(
        x_ref.at[:, :, pl.ds(pl.multiple_of(me * rows, rows), rows)],
        xg_ref.at[:, token_rows], own_sem.at[0])
    own_y = pltpu.make_async_copy(y_ref, yg_ref.at[:, token_rows], own_sem.at[1])
    own_x.start()
    own_y.start()

    if workers > 1:
        part = rows // workers
        mine = pl.ds(pl.multiple_of(worker * part, part), part)
        load_w.wait()
        load_a.wait()
        a_vmem[...] = a_vmem[...] - w_vmem[...]
        drifts, means = [], []
        for d in range(1, workers):
            peer = lax.rem(worker + d, workers)
            drifts.append(pltpu.make_async_remote_copy(
                src_ref=a_vmem.at[pl.ds(pl.multiple_of(peer * part, part), part)],
                dst_ref=slots.at[d - 1],
                send_sem=d_send.at[d - 1], recv_sem=d_recv.at[d - 1],
                device_id=(peer, me), device_id_type=MESH))
        for copy in drifts:
            copy.start()
        if n > 2:
            hop_arrived(1)
            hop_start(2)
        for copy in drifts:
            copy.wait_recv()
        summed = a_vmem[mine]
        for d in range(1, workers):
            summed = summed + slots[d - 1]
        mean[...] = summed / workers
        for d in range(1, workers):
            peer = lax.rem(worker + d, workers)
            means.append(pltpu.make_async_remote_copy(
                src_ref=mean, dst_ref=p_ref.at[mine],
                send_sem=p_send.at[d - 1], recv_sem=p_recv.at[d - 1],
                device_id=(peer, me), device_id_type=MESH))
        for copy in means:
            copy.start()
        own_p = pltpu.make_async_copy(mean, p_ref.at[mine], own_sem.at[2])
        own_p.start()
        pass_on()
        for copy in drifts:
            copy.wait_send()
        for copy in means:
            copy.wait()
        own_p.wait()
    else:
        if n > 2:
            hop_arrived(1)
            hop_start(2)
        pass_on()
    own_x.wait()
    own_y.wait()
    hop_arrived(n - 1)
    for h in range(1, n):
        for way in range(2):
            copy, sends_it, _ = hop(h, way)
            pl.when(sends_it)(copy.wait_send)
    for copy in sends:
        copy.wait()


def exchange(n, workers, inputs, cotangents, weight, anchor):
    steps, tok, din = inputs.shape
    width = cotangents.shape[2]
    rows = din // n
    outs = [
        jax.ShapeDtypeStruct((steps, n * tok, rows), inputs.dtype),
        jax.ShapeDtypeStruct((steps, n * tok, width), cotangents.dtype),
    ]
    operands = [inputs, cotangents]
    near = pltpu.SemaphoreType.DMA((steps, n - 1))
    chain = pltpu.SemaphoreType.DMA((2, n - 1))
    scratch = [near] * 2 + [chain] * 2 + [pltpu.SemaphoreType.DMA((3,))]
    if workers > 1:
        part = rows // workers
        far = pltpu.SemaphoreType.DMA((workers - 1,))
        outs.append(jax.ShapeDtypeStruct((rows, width), F32))
        operands += [weight, anchor]
        scratch = [
            pltpu.VMEM((rows, width), F32),
            pltpu.VMEM((rows, width), F32),
            pltpu.VMEM((workers - 1, part, width), F32),
            pltpu.VMEM((part, width), F32),
        ] + scratch + [pltpu.SemaphoreType.DMA((2,))] + [far] * 4
    return pl.pallas_call(
        functools.partial(exchange_kernel, n, workers),
        out_shape=outs,
        in_specs=[pl.BlockSpec(memory_space=pl.ANY)] * len(operands),
        out_specs=[pl.BlockSpec(memory_space=pl.ANY)] * len(outs),
        scratch_shapes=scratch,
        compiler_params=pltpu.CompilerParams(
            collective_id=0, has_side_effects=True, vmem_limit_bytes=EXCHANGE_VMEM
        ),
        name="exchange",
    )(*operands)


def update_kernel(x_ref, y_ref, w_ref, m_ref, v_ref, a_ref, o_ref, p_ref,
                  w_out, m_out, v_out, a_out, o_out):
    anchor, pseudo = a_ref[...], p_ref[...]
    momentum = MOMENTUM_KEEP * o_ref[...] + pseudo
    anchor_new = anchor - OUTER_RATE * (pseudo + MOMENTUM_KEEP * momentum)
    o_out[...] = momentum
    a_out[...] = anchor_new
    weight, first, second = w_ref[0], m_ref[0], v_ref[0]
    for s in range(x_ref.shape[0]):
        gradient = lax.dot_general(
            x_ref[s], y_ref[s], (((0,), (0,)), ((), ())), preferred_element_type=F32
        )
        first = (BETA_FIRST * first.astype(F32) + (1.0 - BETA_FIRST) * gradient).astype(BF16)
        second = (
            BETA_SECOND * second.astype(F32) + (1.0 - BETA_SECOND) * gradient * gradient
        ).astype(BF16)
        weight = weight - INNER_RATE * (
            first.astype(F32) / (jnp.sqrt(second.astype(F32)) + EPSILON) + WEIGHT_DECAY * weight
        )
        if s == 0:
            weight = MERGE_WEIGHT * weight + (1.0 - MERGE_WEIGHT) * anchor_new
    w_out[0] = weight
    m_out[0] = first
    v_out[0] = second


def update(gathered, upstream, weights, first, second, anchor, outer, pseudo):
    steps, tokens, rows = gathered.shape
    width = upstream.shape[2]
    block = min(256, rows)
    state = pl.BlockSpec((1, block, width), lambda i: (0, i, 0))
    plain = pl.BlockSpec((block, width), lambda i: (i, 0))
    shape = lambda ref: jax.ShapeDtypeStruct(ref.shape, ref.dtype)
    return pl.pallas_call(
        update_kernel,
        grid=(rows // block,),
        in_specs=[
            pl.BlockSpec((steps, tokens, block), lambda i: (0, 0, i)),
            pl.BlockSpec((steps, tokens, width), lambda i: (0, 0, 0)),
            state, state, state, plain, plain, plain,
        ],
        out_specs=[state, state, state, plain, plain],
        out_shape=[shape(weights), shape(first), shape(second), shape(anchor), shape(outer)],
        compiler_params=pltpu.CompilerParams(vmem_limit_bytes=UPDATE_VMEM),
        name="update",
    )(gathered, upstream, weights, first, second, anchor, outer, pseudo)


def solution(mesh):
    n, workers = mesh.shape["fsdp"], mesh.shape["replica"]

    def body(inputs, cotangents, weights, first, second, anchor, outer):
        rows = anchor.shape[0]
        if rows % (16 * workers) == 0:
            gathered, upstream, pseudo = exchange(
                n, workers, inputs, cotangents, weights[0], anchor
            )
        else:
            gathered, upstream = exchange(n, 1, inputs, cotangents, None, None)
            pseudo = lax.psum(anchor - weights[0], "replica") / workers
        return tuple(update(gathered, upstream, weights, first, second, anchor, outer, pseudo))

    in_specs = (
        P(None, ("replica", "fsdp"), None),
        P(None, ("replica", "fsdp"), None),
        P("replica", "fsdp", None),
        P("replica", "fsdp", None),
        P("replica", "fsdp", None),
        P("fsdp", None),
        P("fsdp", None),
    )
    out_specs = (
        P("replica", "fsdp", None),
        P("replica", "fsdp", None),
        P("replica", "fsdp", None),
        P("fsdp", None),
        P("fsdp", None),
    )
    return jax.shard_map(body, mesh=mesh, in_specs=in_specs, out_specs=out_specs, check_vma=False)
```

```python
import functools

import jax
import jax.numpy as jnp
from jax import lax
from jax.experimental import pallas as pl
from jax.experimental.pallas import tpu as pltpu
from jax.sharding import PartitionSpec as P

MESH = pl.DeviceIdType.MESH
F32 = jnp.float32
BF16 = jnp.bfloat16

BETA_FIRST = 0.9
BETA_SECOND = 0.95
INNER_RATE = 0.01
WEIGHT_DECAY = 0.1
EPSILON = 1e-08
OUTER_RATE = 0.7
MOMENTUM_KEEP = 0.9
MERGE_WEIGHT = 0.5
EXCHANGE_VMEM = 52 * 2**20
UPDATE_VMEM = 60 * 2**20
FINISH_VMEM = 28 * 2**20


def greet(n, workers):
    barrier = pltpu.get_barrier_semaphore()
    me, worker = lax.axis_index("fsdp"), lax.axis_index("replica")
    for step in range(1, n):
        pl.semaphore_signal(
            barrier, inc=1, device_id=(worker, lax.rem(me + step, n)), device_id_type=MESH
        )
    for step in range(1, workers):
        pl.semaphore_signal(
            barrier, inc=1, device_id=(lax.rem(worker + step, workers), me), device_id_type=MESH
        )
    pl.semaphore_wait(barrier, n - 1 + workers - 1)


def partner(me, k, n):
    if n & (n - 1):
        return lax.rem(me + k, n)
    peer, bit = me, 1
    while bit < n:
        if k & bit:
            peer = peer + (1 - 2 * (me // bit % 2)) * bit
        bit *= 2
    return peer


def exchange_kernel(n, workers, *refs):
    if workers > 1:
        x_ref, y_ref, *state = refs[:7]
        xg_ref, yg_ref, *held = refs[7:14]
        weight, anchor, first, second, momentum = held
        (drift, slots, pseudo, x_send, x_recv, y_send, y_recv, own_sem, load_sem, d_send, d_recv,
         p_send, p_recv) = refs[14:]
    else:
        x_ref, y_ref, xg_ref, yg_ref, x_send, x_recv, y_send, y_recv, own_sem = refs
    me, worker = lax.axis_index("fsdp"), lax.axis_index("replica")
    steps, tok, din = x_ref.shape
    rows = din // n

    if workers > 1:
        loads = [
            pltpu.make_async_copy(src, dst, load_sem.at[i])
            for i, (src, dst) in enumerate(zip(state, held))
        ]
        for copy in loads:
            copy.start()
    greet(n, workers)

    token_rows = pl.ds(pl.multiple_of(me * tok, tok), tok)
    right, left = lax.rem(me + 1, n), lax.rem(me + n - 1, n)

    def hop(h, way):
        to_right = way == 0
        origin = me - (h - 1) if to_right else me + (h - 1)
        sends_it = jnp.logical_and(origin >= 0, me < n - 1) if to_right else jnp.logical_and(
            origin < n, me > 0)
        comes = me >= h if to_right else me + h < n
        held = pl.ds(pl.multiple_of(lax.rem(origin + n, n) * tok, tok), tok)
        copy = pltpu.make_async_remote_copy(
            src_ref=y_ref if h == 1 else yg_ref.at[:, held], dst_ref=yg_ref.at[:, held],
            send_sem=y_send.at[way, h - 1], recv_sem=y_recv.at[way, h - 1],
            device_id=(worker, right if to_right else left), device_id_type=MESH)
        return copy, sends_it, comes

    def hop_start(h):
        for way in range(2):
            copy, sends_it, _ = hop(h, way)
            pl.when(sends_it)(copy.start)

    def hop_arrived(h):
        for way in range(2):
            copy, _, comes = hop(h, way)
            pl.when(comes)(copy.wait_recv)

    def pass_on():
        for h in range(3, n):
            hop_arrived(h - 1)
            hop_start(h)

    hop_start(1)
    sends = []
    for s in range(steps):
        for k in range(n - 1, 0, -1):
            peer = partner(me, k, n)
            sends.append(pltpu.make_async_remote_copy(
                src_ref=x_ref.at[s, :, pl.ds(pl.multiple_of(peer * rows, rows), rows)],
                dst_ref=xg_ref.at[s, token_rows],
                send_sem=x_send.at[s, k - 1], recv_sem=x_recv.at[s, k - 1],
                device_id=(worker, peer), device_id_type=MESH))
    for copy in (sends[:n - 1] if workers > 1 else sends):
        copy.start()
    own_x = pltpu.make_async_copy(
        x_ref.at[:, :, pl.ds(pl.multiple_of(me * rows, rows), rows)],
        xg_ref.at[:, token_rows], own_sem.at[0])
    own_y = pltpu.make_async_copy(y_ref, yg_ref.at[:, token_rows], own_sem.at[1])
    own_x.start()
    own_y.start()

    if workers > 1:
        part = rows // workers
        mine = pl.ds(pl.multiple_of(worker * part, part), part)
        loads[0].wait()
        loads[1].wait()
        drift[...] = anchor[...] - weight[...]
        drifts, means = [], []
        for d in range(1, workers):
            peer = lax.rem(worker + d, workers)
            drifts.append(pltpu.make_async_remote_copy(
                src_ref=drift.at[pl.ds(pl.multiple_of(peer * part, part), part)],
                dst_ref=slots.at[d - 1],
                send_sem=d_send.at[d - 1], recv_sem=d_recv.at[d - 1],
                device_id=(peer, me), device_id_type=MESH))
        for copy in drifts:
            copy.start()
        if n > 2:
            hop_arrived(1)
            hop_start(2)
        sends[0].wait_send()
        sends[n - 1].start()
        for copy in drifts:
            copy.wait_recv()
        summed = drift[mine]
        for d in range(1, workers):
            summed = summed + slots[d - 1]
        pseudo[mine] = summed / workers
        for d in range(1, workers):
            peer = lax.rem(worker + d, workers)
            means.append(pltpu.make_async_remote_copy(
                src_ref=pseudo.at[mine], dst_ref=pseudo.at[mine],
                send_sem=p_send.at[d - 1], recv_sem=p_recv.at[d - 1],
                device_id=(peer, me), device_id_type=MESH))
        for copy in means:
            copy.start()
        for copy in sends[1:n - 1]:
            copy.wait_send()
        for copy in sends[n:]:
            copy.start()
        pass_on()
        for copy in loads[2:]:
            copy.wait()
        own_x.wait()
        own_y.wait()
        hop_arrived(n - 1)
        for copy in sends[:n - 1]:
            copy.wait_recv()
        for copy in means:
            copy.wait_recv()
        block = min(128, rows)

        @pl.loop(0, rows // block)
        def _(i):
            at = pl.ds(pl.multiple_of(i * block, block), block)
            weight[at], first[at], second[at] = inner(
                xg_ref[0, :, at], yg_ref[0], weight[at], first[at], second[at])
            mean = pseudo[at]
            kept = MOMENTUM_KEEP * momentum[at] + mean
            momentum[at] = kept
            merged = anchor[at] - OUTER_RATE * (mean + MOMENTUM_KEEP * kept)
            anchor[at] = merged
            weight[at] = MERGE_WEIGHT * weight[at] + (1.0 - MERGE_WEIGHT) * merged

        for copy in drifts + means:
            copy.wait_send()
        for copy in sends[n - 1:]:
            copy.wait()
    else:
        if n > 2:
            hop_arrived(1)
            hop_start(2)
        pass_on()
        own_x.wait()
        own_y.wait()
        hop_arrived(n - 1)
        for copy in sends:
            copy.wait()
    for h in range(1, n):
        for way in range(2):
            copy, sends_it, _ = hop(h, way)
            pl.when(sends_it)(copy.wait_send)


def inner(features, upstream, weight, first, second):
    gradient = lax.dot_general(
        features, upstream, (((0,), (0,)), ((), ())), preferred_element_type=F32
    )
    first = (BETA_FIRST * first.astype(F32) + (1.0 - BETA_FIRST) * gradient).astype(BF16)
    second = (
        BETA_SECOND * second.astype(F32) + (1.0 - BETA_SECOND) * gradient * gradient
    ).astype(BF16)
    weight = weight - INNER_RATE * (
        first.astype(F32) / (jnp.sqrt(second.astype(F32)) + EPSILON) + WEIGHT_DECAY * weight
    )
    return weight, first, second


def exchange(n, workers, inputs, cotangents, *state):
    steps, tok, din = inputs.shape
    width = cotangents.shape[2]
    rows = din // n
    outs = [
        jax.ShapeDtypeStruct((steps, n * tok, rows), inputs.dtype),
        jax.ShapeDtypeStruct((steps, n * tok, width), cotangents.dtype),
    ]
    operands = [inputs, cotangents]
    near = pltpu.SemaphoreType.DMA((steps, n - 1))
    chain = pltpu.SemaphoreType.DMA((2, n - 1))
    scratch = [near] * 2 + [chain] * 2 + [pltpu.SemaphoreType.DMA((3,))]
    if workers > 1:
        part = rows // workers
        far = pltpu.SemaphoreType.DMA((workers - 1,))
        outs = [pltpu.VMEM(out.shape, out.dtype) for out in outs + list(state)]
        operands += state
        scratch = [
            pltpu.VMEM((rows, width), F32),
            pltpu.VMEM((workers - 1, part, width), F32),
            pltpu.VMEM((rows, width), F32),
        ] + scratch + [pltpu.SemaphoreType.DMA((5,))] + [far] * 4
    return pl.pallas_call(
        functools.partial(exchange_kernel, n, workers),
        out_shape=outs,
        in_specs=[pl.BlockSpec(memory_space=pl.ANY)] * len(operands),
        out_specs=[pl.BlockSpec(memory_space=pltpu.VMEM if workers > 1 else pl.ANY)] * len(outs),
        scratch_shapes=scratch,
        compiler_params=pltpu.CompilerParams(
            collective_id=0, has_side_effects=True, vmem_limit_bytes=EXCHANGE_VMEM
        ),
        name="exchange",
    )(*operands)


def update_kernel(x_ref, y_ref, w_ref, m_ref, v_ref, a_ref, o_ref, p_ref,
                  w_out, m_out, v_out, a_out, o_out):
    anchor, pseudo = a_ref[...], p_ref[...]
    momentum = MOMENTUM_KEEP * o_ref[...] + pseudo
    anchor_new = anchor - OUTER_RATE * (pseudo + MOMENTUM_KEEP * momentum)
    o_out[...] = momentum
    a_out[...] = anchor_new
    weight, first, second = w_ref[0], m_ref[0], v_ref[0]
    for s in range(x_ref.shape[0]):
        weight, first, second = inner(x_ref[s], y_ref[s], weight, first, second)
        if s == 0:
            weight = MERGE_WEIGHT * weight + (1.0 - MERGE_WEIGHT) * anchor_new
    w_out[0] = weight
    m_out[0] = first
    v_out[0] = second


def update(gathered, upstream, weights, first, second, anchor, outer, pseudo):
    steps, tokens, rows = gathered.shape
    width = upstream.shape[2]
    block = min(256, rows)
    state = pl.BlockSpec((1, block, width), lambda i: (0, i, 0))
    plain = pl.BlockSpec((block, width), lambda i: (i, 0))
    shape = lambda ref: jax.ShapeDtypeStruct(ref.shape, ref.dtype)
    return pl.pallas_call(
        update_kernel,
        grid=(rows // block,),
        in_specs=[
            pl.BlockSpec((steps, tokens, block), lambda i: (0, 0, i)),
            pl.BlockSpec((steps, tokens, width), lambda i: (0, 0, 0)),
            state, state, state, plain, plain, plain,
        ],
        out_specs=[state, state, state, plain, plain],
        out_shape=[shape(weights), shape(first), shape(second), shape(anchor), shape(outer)],
        compiler_params=pltpu.CompilerParams(vmem_limit_bytes=UPDATE_VMEM),
        name="update",
    )(gathered, upstream, weights, first, second, anchor, outer, pseudo)


def finish_kernel(x_ref, y_ref, w_ref, a_ref, m_ref, v_ref, o_ref, w_out, m_out, v_out, a_out, o_out):
    o_out[...] = o_ref[...]
    a_out[...] = a_ref[...]
    weight, first, second = w_ref[...], m_ref[...], v_ref[...]
    for s in range(x_ref.shape[0]):
        weight, first, second = inner(x_ref[s], y_ref[s], weight, first, second)
    w_out[0] = weight
    m_out[0] = first
    v_out[0] = second


def finish(gathered, upstream, weight, anchor, first, second, momentum):
    steps, tokens, rows = gathered.shape
    width = upstream.shape[2]
    block = min(256, rows)
    state = pl.BlockSpec((1, block, width), lambda i: (0, i, 0))
    plain = pl.BlockSpec((block, width), lambda i: (i, 0))
    shape = lambda ref: jax.ShapeDtypeStruct(ref.shape, ref.dtype)
    lead = lambda ref: jax.ShapeDtypeStruct((1,) + ref.shape, ref.dtype)
    later = steps - 1
    return pl.pallas_call(
        finish_kernel,
        grid=(rows // block,),
        in_specs=[
            pl.BlockSpec((later, tokens, block), lambda i: (1, 0, i)),
            pl.BlockSpec((later, tokens, width), lambda i: (1, 0, 0)),
            plain, plain, plain, plain, plain,
        ],
        out_specs=[state, state, state, plain, plain],
        out_shape=[lead(weight), lead(first), lead(second), shape(anchor), shape(momentum)],
        compiler_params=pltpu.CompilerParams(vmem_limit_bytes=FINISH_VMEM),
        name="finish",
    )(gathered, upstream, weight, anchor, first, second, momentum)


def solution(mesh):
    n, workers = mesh.shape["fsdp"], mesh.shape["replica"]

    def body(inputs, cotangents, weights, first, second, anchor, outer):
        rows = anchor.shape[0]
        if rows % (16 * workers) == 0 and inputs.shape[0] == 2:
            return tuple(finish(*exchange(
                n, workers, inputs, cotangents, weights[0], anchor, first[0], second[0], outer
            )))
        gathered, upstream = exchange(n, 1, inputs, cotangents)
        pseudo = lax.psum(anchor - weights[0], "replica") / workers
        return tuple(update(gathered, upstream, weights, first, second, anchor, outer, pseudo))

    in_specs = (
        P(None, ("replica", "fsdp"), None),
        P(None, ("replica", "fsdp"), None),
        P("replica", "fsdp", None),
        P("replica", "fsdp", None),
        P("replica", "fsdp", None),
        P("fsdp", None),
        P("fsdp", None),
    )
    out_specs = (
        P("replica", "fsdp", None),
        P("replica", "fsdp", None),
        P("replica", "fsdp", None),
        P("fsdp", None),
        P("fsdp", None),
    )
    return jax.shard_map(body, mesh=mesh, in_specs=in_specs, out_specs=out_specs, check_vma=False)
```

```python
import functools

import jax
import jax.numpy as jnp
from jax import lax
from jax.experimental import pallas as pl
from jax.experimental.pallas import tpu as pltpu
from jax.sharding import PartitionSpec as P

MESH = pl.DeviceIdType.MESH
F32 = jnp.float32
BF16 = jnp.bfloat16

BETA_FIRST = 0.9
BETA_SECOND = 0.95
INNER_RATE = 0.01
WEIGHT_DECAY = 0.1
EPSILON = 1e-08
OUTER_RATE = 0.7
MOMENTUM_KEEP = 0.9
MERGE_WEIGHT = 0.5
EXCHANGE_VMEM = 52 * 2**20
UPDATE_VMEM = 60 * 2**20
FINISH_VMEM = 28 * 2**20


def greet(n, workers):
    barrier = pltpu.get_barrier_semaphore()
    me, worker = lax.axis_index("fsdp"), lax.axis_index("replica")
    for step in range(1, n):
        pl.semaphore_signal(
            barrier, inc=1, device_id=(worker, lax.rem(me + step, n)), device_id_type=MESH
        )
    for step in range(1, workers):
        pl.semaphore_signal(
            barrier, inc=1, device_id=(lax.rem(worker + step, workers), me), device_id_type=MESH
        )
    pl.semaphore_wait(barrier, n - 1 + workers - 1)


def partner(me, k, n):
    if n & (n - 1):
        return lax.rem(me + k, n)
    peer, bit = me, 1
    while bit < n:
        if k & bit:
            peer = peer + (1 - 2 * (me // bit % 2)) * bit
        bit *= 2
    return peer


def exchange_kernel(n, workers, *refs):
    if workers > 1:
        x_ref, y_ref, *state = refs[:7]
        xg_ref, yg_ref, *held = refs[7:14]
        weight, anchor, first, second, momentum = held
        (drift, slots, pseudo, x_send, x_recv, y_send, y_recv, own_sem, load_sem, d_send, d_recv,
         p_send, p_recv) = refs[14:]
    else:
        x_ref, y_ref, xg_ref, yg_ref, x_send, x_recv, y_send, y_recv, own_sem = refs
    me, worker = lax.axis_index("fsdp"), lax.axis_index("replica")
    steps, tok, din = x_ref.shape
    rows = din // n

    if workers > 1:
        loads = [
            pltpu.make_async_copy(src, dst, load_sem.at[i])
            for i, (src, dst) in enumerate(zip(state, held))
        ]
        for copy in loads:
            copy.start()
    greet(n, workers)

    token_rows = pl.ds(pl.multiple_of(me * tok, tok), tok)
    right, left = lax.rem(me + 1, n), lax.rem(me + n - 1, n)

    def hop(h, way):
        to_right = way == 0
        origin = me - (h - 1) if to_right else me + (h - 1)
        sends_it = jnp.logical_and(origin >= 0, me < n - 1) if to_right else jnp.logical_and(
            origin < n, me > 0)
        comes = me >= h if to_right else me + h < n
        held = pl.ds(pl.multiple_of(lax.rem(origin + n, n) * tok, tok), tok)
        copy = pltpu.make_async_remote_copy(
            src_ref=y_ref if h == 1 else yg_ref.at[:, held], dst_ref=yg_ref.at[:, held],
            send_sem=y_send.at[way, h - 1], recv_sem=y_recv.at[way, h - 1],
            device_id=(worker, right if to_right else left), device_id_type=MESH)
        return copy, sends_it, comes

    def hop_start(h):
        for way in range(2):
            copy, sends_it, _ = hop(h, way)
            pl.when(sends_it)(copy.start)

    def hop_arrived(h):
        for way in range(2):
            copy, _, comes = hop(h, way)
            pl.when(comes)(copy.wait_recv)

    def pass_on():
        for h in range(3, n):
            hop_arrived(h - 1)
            hop_start(h)

    hop_start(1)
    sends = []
    for s in range(steps):
        for k in range(n - 1, 0, -1):
            peer = partner(me, k, n)
            sends.append(pltpu.make_async_remote_copy(
                src_ref=x_ref.at[s, :, pl.ds(pl.multiple_of(peer * rows, rows), rows)],
                dst_ref=xg_ref.at[s, token_rows],
                send_sem=x_send.at[s, k - 1], recv_sem=x_recv.at[s, k - 1],
                device_id=(worker, peer), device_id_type=MESH))
    for copy in (sends[:n - 1] if workers > 1 else sends):
        copy.start()
    own_x = pltpu.make_async_copy(
        x_ref.at[:, :, pl.ds(pl.multiple_of(me * rows, rows), rows)],
        xg_ref.at[:, token_rows], own_sem.at[0])
    own_y = pltpu.make_async_copy(y_ref, yg_ref.at[:, token_rows], own_sem.at[1])
    own_x.start()
    own_y.start()

    if workers > 1:
        part = rows // workers
        mine = pl.ds(pl.multiple_of(worker * part, part), part)
        loads[0].wait()
        loads[1].wait()
        drift[...] = anchor[...] - weight[...]
        drifts, means = [], []
        for d in range(1, workers):
            peer = lax.rem(worker + d, workers)
            drifts.append(pltpu.make_async_remote_copy(
                src_ref=drift.at[pl.ds(pl.multiple_of(peer * part, part), part)],
                dst_ref=slots.at[d - 1],
                send_sem=d_send.at[d - 1], recv_sem=d_recv.at[d - 1],
                device_id=(peer, me), device_id_type=MESH))
        for copy in drifts:
            copy.start()
        if n > 2:
            hop_arrived(1)
            hop_start(2)
        for copy in drifts:
            copy.wait_recv()
        summed = drift[mine]
        for d in range(1, workers):
            summed = summed + slots[d - 1]
        pseudo[mine] = summed / workers
        for d in range(1, workers):
            peer = lax.rem(worker + d, workers)
            means.append(pltpu.make_async_remote_copy(
                src_ref=pseudo.at[mine], dst_ref=pseudo.at[mine],
                send_sem=p_send.at[d - 1], recv_sem=p_recv.at[d - 1],
                device_id=(peer, me), device_id_type=MESH))
        for copy in means:
            copy.start()
        for copy, later in zip(sends[:n - 1], sends[n - 1:]):
            copy.wait_send()
            later.start()
        pass_on()
        for copy in loads[2:]:
            copy.wait()
        own_x.wait()
        own_y.wait()
        hop_arrived(n - 1)
        for copy in sends[:n - 1]:
            copy.wait_recv()
        for copy in means:
            copy.wait_recv()
        block = min(128, rows)

        @pl.loop(0, rows // block)
        def _(i):
            at = pl.ds(pl.multiple_of(i * block, block), block)
            weight[at], first[at], second[at] = inner(
                xg_ref[0, :, at], yg_ref[0], weight[at], first[at], second[at])
            mean = pseudo[at]
            kept = MOMENTUM_KEEP * momentum[at] + mean
            momentum[at] = kept
            merged = anchor[at] - OUTER_RATE * (mean + MOMENTUM_KEEP * kept)
            anchor[at] = merged
            weight[at] = MERGE_WEIGHT * weight[at] + (1.0 - MERGE_WEIGHT) * merged

        for copy in drifts + means:
            copy.wait_send()
        for copy in sends[n - 1:]:
            copy.wait()
    else:
        if n > 2:
            hop_arrived(1)
            hop_start(2)
        pass_on()
        own_x.wait()
        own_y.wait()
        hop_arrived(n - 1)
        for copy in sends:
            copy.wait()
    for h in range(1, n):
        for way in range(2):
            copy, sends_it, _ = hop(h, way)
            pl.when(sends_it)(copy.wait_send)


def inner(features, upstream, weight, first, second):
    gradient = lax.dot_general(
        features, upstream, (((0,), (0,)), ((), ())), preferred_element_type=F32
    )
    first = (BETA_FIRST * first.astype(F32) + (1.0 - BETA_FIRST) * gradient).astype(BF16)
    second = (
        BETA_SECOND * second.astype(F32) + (1.0 - BETA_SECOND) * gradient * gradient
    ).astype(BF16)
    weight = weight - INNER_RATE * (
        first.astype(F32) / (jnp.sqrt(second.astype(F32)) + EPSILON) + WEIGHT_DECAY * weight
    )
    return weight, first, second


def exchange(n, workers, inputs, cotangents, *state):
    steps, tok, din = inputs.shape
    width = cotangents.shape[2]
    rows = din // n
    outs = [
        jax.ShapeDtypeStruct((steps, n * tok, rows), inputs.dtype),
        jax.ShapeDtypeStruct((steps, n * tok, width), cotangents.dtype),
    ]
    operands = [inputs, cotangents]
    near = pltpu.SemaphoreType.DMA((steps, n - 1))
    chain = pltpu.SemaphoreType.DMA((2, n - 1))
    scratch = [near] * 2 + [chain] * 2 + [pltpu.SemaphoreType.DMA((3,))]
    if workers > 1:
        part = rows // workers
        far = pltpu.SemaphoreType.DMA((workers - 1,))
        outs = [pltpu.VMEM(out.shape, out.dtype) for out in outs + list(state)]
        operands += state
        scratch = [
            pltpu.VMEM((rows, width), F32),
            pltpu.VMEM((workers - 1, part, width), F32),
            pltpu.VMEM((rows, width), F32),
        ] + scratch + [pltpu.SemaphoreType.DMA((5,))] + [far] * 4
    return pl.pallas_call(
        functools.partial(exchange_kernel, n, workers),
        out_shape=outs,
        in_specs=[pl.BlockSpec(memory_space=pl.ANY)] * len(operands),
        out_specs=[pl.BlockSpec(memory_space=pltpu.VMEM if workers > 1 else pl.ANY)] * len(outs),
        scratch_shapes=scratch,
        compiler_params=pltpu.CompilerParams(
            collective_id=0, has_side_effects=True, vmem_limit_bytes=EXCHANGE_VMEM
        ),
        name="exchange",
    )(*operands)


def update_kernel(x_ref, y_ref, w_ref, m_ref, v_ref, a_ref, o_ref, p_ref,
                  w_out, m_out, v_out, a_out, o_out):
    anchor, pseudo = a_ref[...], p_ref[...]
    momentum = MOMENTUM_KEEP * o_ref[...] + pseudo
    anchor_new = anchor - OUTER_RATE * (pseudo + MOMENTUM_KEEP * momentum)
    o_out[...] = momentum
    a_out[...] = anchor_new
    weight, first, second = w_ref[0], m_ref[0], v_ref[0]
    for s in range(x_ref.shape[0]):
        weight, first, second = inner(x_ref[s], y_ref[s], weight, first, second)
        if s == 0:
            weight = MERGE_WEIGHT * weight + (1.0 - MERGE_WEIGHT) * anchor_new
    w_out[0] = weight
    m_out[0] = first
    v_out[0] = second


def update(gathered, upstream, weights, first, second, anchor, outer, pseudo):
    steps, tokens, rows = gathered.shape
    width = upstream.shape[2]
    block = min(256, rows)
    state = pl.BlockSpec((1, block, width), lambda i: (0, i, 0))
    plain = pl.BlockSpec((block, width), lambda i: (i, 0))
    shape = lambda ref: jax.ShapeDtypeStruct(ref.shape, ref.dtype)
    return pl.pallas_call(
        update_kernel,
        grid=(rows // block,),
        in_specs=[
            pl.BlockSpec((steps, tokens, block), lambda i: (0, 0, i)),
            pl.BlockSpec((steps, tokens, width), lambda i: (0, 0, 0)),
            state, state, state, plain, plain, plain,
        ],
        out_specs=[state, state, state, plain, plain],
        out_shape=[shape(weights), shape(first), shape(second), shape(anchor), shape(outer)],
        compiler_params=pltpu.CompilerParams(vmem_limit_bytes=UPDATE_VMEM),
        name="update",
    )(gathered, upstream, weights, first, second, anchor, outer, pseudo)


def finish_kernel(x_ref, y_ref, w_ref, a_ref, m_ref, v_ref, o_ref, w_out, m_out, v_out, a_out, o_out):
    o_out[...] = o_ref[...]
    a_out[...] = a_ref[...]
    weight, first, second = w_ref[...], m_ref[...], v_ref[...]
    for s in range(x_ref.shape[0]):
        weight, first, second = inner(x_ref[s], y_ref[s], weight, first, second)
    w_out[0] = weight
    m_out[0] = first
    v_out[0] = second


def finish(gathered, upstream, weight, anchor, first, second, momentum):
    steps, tokens, rows = gathered.shape
    width = upstream.shape[2]
    block = min(512, rows)
    state = pl.BlockSpec((1, block, width), lambda i: (0, i, 0))
    plain = pl.BlockSpec((block, width), lambda i: (i, 0))
    shape = lambda ref: jax.ShapeDtypeStruct(ref.shape, ref.dtype)
    lead = lambda ref: jax.ShapeDtypeStruct((1,) + ref.shape, ref.dtype)
    later = steps - 1
    return pl.pallas_call(
        finish_kernel,
        grid=(rows // block,),
        in_specs=[
            pl.BlockSpec((later, tokens, block), lambda i: (1, 0, i)),
            pl.BlockSpec((later, tokens, width), lambda i: (1, 0, 0)),
            plain, plain, plain, plain, plain,
        ],
        out_specs=[state, state, state, plain, plain],
        out_shape=[lead(weight), lead(first), lead(second), shape(anchor), shape(momentum)],
        compiler_params=pltpu.CompilerParams(vmem_limit_bytes=FINISH_VMEM),
        name="finish",
    )(gathered, upstream, weight, anchor, first, second, momentum)


def solution(mesh):
    n, workers = mesh.shape["fsdp"], mesh.shape["replica"]

    def body(inputs, cotangents, weights, first, second, anchor, outer):
        rows = anchor.shape[0]
        if rows % (16 * workers) == 0 and inputs.shape[0] == 2:
            return tuple(finish(*exchange(
                n, workers, inputs, cotangents, weights[0], anchor, first[0], second[0], outer
            )))
        gathered, upstream = exchange(n, 1, inputs, cotangents)
        pseudo = lax.psum(anchor - weights[0], "replica") / workers
        return tuple(update(gathered, upstream, weights, first, second, anchor, outer, pseudo))

    in_specs = (
        P(None, ("replica", "fsdp"), None),
        P(None, ("replica", "fsdp"), None),
        P("replica", "fsdp", None),
        P("replica", "fsdp", None),
        P("replica", "fsdp", None),
        P("fsdp", None),
        P("fsdp", None),
    )
    out_specs = (
        P("replica", "fsdp", None),
        P("replica", "fsdp", None),
        P("replica", "fsdp", None),
        P("fsdp", None),
        P("fsdp", None),
    )
    return jax.shard_map(body, mesh=mesh, in_specs=in_specs, out_specs=out_specs, check_vma=False)
```
